512 devices in a mesh: req: 4 (over x), head: 8 (over y, core), ctx: 16 (over z).
Axes of the slice: x: 4, y: 4, z: 16, core: 2. Of those that a mesh axis runs over, the one named last changes fastest.
Arguments:
- queries: bfloat16 [32768, 2048], P(('req', 'ctx'), 'head'), parts along dimension 0, may hold values from -8 to 8
- keys_own: bfloat16 [32768, 2048], P(('req', 'ctx'), 'head'), parts along dimension 0, may hold values from -8 to 8
- values_own: bfloat16 [32768, 2048], P(('req', 'ctx'), 'head'), parts along dimension 0, may hold values from -6 to 6
- keys_cache: bfloat16 [262144, 2048], P(('req', 'ctx'), 'head'), parts along dimension 0, may hold values from -8 to 8
- values_cache: bfloat16 [262144, 2048], P(('req', 'ctx'), 'head'), parts along dimension 0, may hold values from -6 to 6
- picks: int32 [64, 16, 3], P(('req', 'ctx'), 'head'), parts along dimension 0, may hold values from 0 to 15, as said below
Outputs:
- attended: bfloat16 [32768, 2048], P(('req', 'ctx'), 'head'), parts along dimension 0
The draws below stay inside these ranges and needn't reach their ends.
There are 4 independent parts, one for each index of `req`. The reference program is written for one: setup_inputs(seed, part) draws one part's arguments, and reference() takes and returns one part's arrays. A program takes and returns all parts, laid end to end along the dimension named above; each array names one. Nothing has to cross between parts.
Inputs may be any that keep to these rules, and one draw needn't show every extreme that they name: Block b is stored on ctx index b. The 3 picks of one tile and head name blocks on different ctx indices. Among the picks of one tile over the 2 heads of one head index, at most 1 name blocks on any one ctx index, and exactly 1 do for a ctx index that is the same for all tiles.
All inputs are finite; a program needn't handle non-finite values.
Results may differ from the reference program's by a relative error of at most 0.0048.
Values may be sent and summed in bfloat16 or wider, within the bound.
A program may use at most 64 MiB of HBM per device.

```python
import jax
import jax.numpy as jnp
from jax import lax

HDIM = 128
HEADS_DEV = 2
TILE = 512
BLOCK = 4096
TOPK = 3
BLK_DEV = 1
HEADS = 16
OWNERS = 16
TOKENS = 8192
NBLK = 16
CACHE = 65536


def normal_rows(key, rows):
    return jnp.clip(jax.random.normal(key, (rows, HEADS * HDIM), jnp.float32), -4.0, 4.0).astype(jnp.bfloat16)


def draw_queries(key, part):
    key = jax.random.fold_in(key, 1)
    return normal_rows(key, TOKENS)


def draw_keys_own(key, part):
    key = jax.random.fold_in(key, 2)
    return normal_rows(key, TOKENS)


def draw_keys_cache(key, part):
    key = jax.random.fold_in(key, 3)
    return normal_rows(key, CACHE)


def draw_picks(key, part):
    key = jax.random.fold_in(key, 11)
    hottest = jax.random.randint(jax.random.fold_in(key, 0), (), 0, OWNERS)
    groups = HEADS // HEADS_DEV
    pick_count = HEADS_DEV * TOPK
    device_keys = jax.random.split(jax.random.fold_in(key, 1), groups * OWNERS)

    def device_table(device_key):
        key_order, key_local, key_heads, key_slots = jax.random.split(device_key, 4)
        others = (hottest + 1 + jax.random.permutation(key_order, OWNERS - 1)) % OWNERS
        order = jnp.concatenate([hottest[None], others]).astype(jnp.int32)
        serial = jnp.arange(pick_count, dtype=jnp.int32)
        owner = order[serial % OWNERS]
        local = jax.random.randint(key_local, (pick_count,), 0, BLK_DEV)
        blocks = (owner * BLK_DEV + local).reshape(HEADS_DEV, TOPK)
        blocks = blocks[jax.random.permutation(key_heads, HEADS_DEV)]
        ranking = jax.random.randint(key_slots, (HEADS_DEV, TOPK), 0, 1 << 20) * TOPK + jnp.arange(TOPK, dtype=jnp.int32)[None, :]
        return jnp.take_along_axis(blocks, jnp.argsort(ranking, axis=1), axis=1)
    table = jax.vmap(device_table)(device_keys).reshape(groups, OWNERS, HEADS_DEV, TOPK)
    return table.transpose(1, 0, 2, 3).reshape(OWNERS, HEADS, TOPK).astype(jnp.int32)


def levels(own_key, dims, cuts, least, top_value):
    def one(axis_at, blocks):
        steps = jax.random.uniform(jax.random.fold_in(jax.random.fold_in(own_key, 6), axis_at), (blocks,), jnp.float32, least / len(cuts), top_value / len(cuts))
        return jnp.repeat(jnp.exp(steps), dims[axis_at] // blocks).reshape((-1,) + (1,) * (len(dims) - axis_at - 1))

    loudness = one(*cuts[0])
    for cut in cuts[1:]:
        loudness = loudness * one(*cut)
    return loudness


def scatter_about(stream_key, extent, width, most, cuts=(), kind=jnp.bfloat16):
    values = jax.random.normal(stream_key, extent, jnp.float32) * width
    if len(cuts) > 0:
        values = levels(stream_key, extent, cuts, -0.22, 0.18) * values
    return jnp.clip(values, min=-most, max=most).astype(kind)


def setup_inputs(seed: int = 0, part: int = 0) -> dict:
    seeds = jax.random.split(jax.random.key(seed), 7)
    own_keys = jax.random.split(jax.random.fold_in(seeds[6], part), 7)
    queries = draw_queries(jax.random.fold_in(jax.random.fold_in(seeds[6], part), 71), part)
    keys_own = draw_keys_own(jax.random.fold_in(jax.random.fold_in(seeds[6], part), 71), part)
    values_own = scatter_about(own_keys[2], (TOKENS, HEADS * HDIM), 1.0, 6.0, ((0, 16), (1, 8)))
    keys_cache = draw_keys_cache(jax.random.fold_in(jax.random.fold_in(seeds[6], part), 71), part)
    values_cache = scatter_about(own_keys[4], (CACHE, HEADS * HDIM), 1.0, 6.0, ((0, 16), (1, 8)))
    picks = draw_picks(jax.random.fold_in(jax.random.fold_in(seeds[6], part), 71), part)
    return {"queries": queries, "keys_own": keys_own, "values_own": values_own, "keys_cache": keys_cache, "values_cache": values_cache, "picks": picks}


NEG = -1e30


def attend(query, keys, values, bias):
    scores = lax.dot_general(query, keys, (((1,), (1,)), ((), ())), preferred_element_type=jnp.float32) * (query.shape[-1] ** -0.5) + bias
    top = jnp.max(scores, axis=-1)
    expo = jnp.exp(scores - top[:, None])
    total = jnp.sum(expo, axis=-1)
    summed = jnp.dot(expo.astype(jnp.bfloat16), values, preferred_element_type=jnp.float32)
    return summed, top, total


def combine(summed, top, total):
    best = jnp.max(top, axis=0)
    factor = jnp.exp(top - best[None])
    numer = jnp.sum(summed * factor[..., None], axis=0)
    denom = jnp.sum(total * factor, axis=0)
    return (numer / denom[..., None]).astype(jnp.bfloat16)


def reference(queries, keys_own, values_own, keys_cache, values_cache, picks):
    query_tiles = queries.reshape(OWNERS, TILE, HEADS, HDIM).transpose(0, 2, 1, 3)
    key_tiles = keys_own.reshape(OWNERS, TILE, HEADS, HDIM).transpose(0, 2, 1, 3)
    value_tiles = values_own.reshape(OWNERS, TILE, HEADS, HDIM).transpose(0, 2, 1, 3)
    cache_keys = keys_cache.reshape(NBLK, BLOCK, HEADS, HDIM)
    cache_values = values_cache.reshape(NBLK, BLOCK, HEADS, HDIM)
    position = jnp.arange(TILE)
    causal = jnp.where(position[:, None] >= position[None, :], 0.0, NEG).astype(jnp.float32)
    zero_bias = jnp.zeros((), jnp.float32)

    def per_head(head, query, keys, values, chosen):
        parts = [attend(query, keys, values, causal)]
        for slot in range(TOPK):
            block_keys = cache_keys[chosen[slot], :, head, :]
            block_values = cache_values[chosen[slot], :, head, :]
            parts.append(attend(query, block_keys, block_values, zero_bias))
        summed = jnp.stack([part[0] for part in parts])
        top = jnp.stack([part[1] for part in parts])
        total = jnp.stack([part[2] for part in parts])
        return combine(summed, top, total)

    def per_tile(pieces):
        query, keys, values, chosen = pieces
        heads_index = jnp.arange(HEADS, dtype=jnp.int32)
        return jax.vmap(per_head)(heads_index, query, keys, values, chosen)

    result = lax.map(per_tile, (query_tiles, key_tiles, value_tiles, picks))
    return result.transpose(0, 2, 1, 3).reshape(TOKENS, HEADS * HDIM)
```

```python
import functools
import math

import jax
import jax.numpy as jnp
from jax import lax
from jax.experimental import pallas as pl
from jax.experimental.pallas import tpu as pltpu
from jax.sharding import PartitionSpec as P

NEG = -1e30
LANES = 128
CHUNK = 1024
PIECE = 512
STRIP = 64
UNROLL = 2
NEAR = 6
FAR7 = (13, 15)
FAR8 = 14
WAVES = 1
UNITS = 2 * NEAR + 4
MESH = pl.DeviceIdType.MESH
F32 = jnp.float32
BF16 = jnp.bfloat16


def matmul(a, b):
    return lax.dot_general(a, b, (((1,), (0,)), ((), ())), preferred_element_type=F32)


def against(a, b):
    return lax.dot_general(a, b, (((1,), (1,)), ((), ())), preferred_element_type=F32)


def flipped(x):
    width = x.shape[1]
    rows = lax.broadcasted_iota(jnp.int32, (width, width), 0)
    columns = lax.broadcasted_iota(jnp.int32, (width, width), 1)
    eye = jnp.where(rows == columns, 1.0, 0.0).astype(BF16)
    return against(eye, x).astype(BF16)


def fold(x, op):
    return op(x.reshape(x.shape[0] // 8, 8, x.shape[1]), axis=0)


def mix(o1, l1, o2, l2):
    best = jnp.maximum(l1, l2)
    a = jnp.exp2(l1 - best)
    b = jnp.exp2(l2 - best)
    total = a + b
    part = 1.0 / total
    return o1 * (a * part) + o2 * (b * part), best + jnp.log2(total)


def slot(side, d):
    return 2 * d - 1 + side


def kernel(
    ranks, rate,
    picks, q_in, ko_in, vo_in, k_in, v_in,
    out,
    q_own, k_own, v_own, vt_own, keys, values, kt, vw,
    qt, tab, qm, s_a, s_b, m_a, m_b, acc,
    part, plse, mine, mlse,
    sel7, sel8, pass8,
    od8, od7, a8, a8l, b8, b8l, b7, b7l, chain, clse,
    load_sem, q_send, q_recv, t_send, t_recv, f_send, f_recv, c_send, c_recv,
):
    z = lax.axis_index("ctx")
    after = lax.rem(z + 1, ranks)
    before = lax.rem(z + ranks - 1, ranks)
    rows = q_own.shape[0]
    span = rows // WAVES
    blocks = span // LANES
    half = blocks // 2
    n_chunks = keys.shape[0] // CHUNK
    lane = lax.broadcasted_iota(jnp.int32, (8, LANES), 1)

    loads = [
        pltpu.make_async_copy(source, target, load_sem.at[i])
        for i, (source, target) in enumerate(
            [(q_in, q_own), (k_in, keys), (v_in, values), (ko_in, k_own), (vo_in, v_own)]
        )
    ]
    for load in loads:
        load.start()

    barrier = pltpu.get_barrier_semaphore()
    for peer in (before, after):
        pl.semaphore_signal(barrier, inc=1, device_id={"ctx": peer}, device_id_type=MESH)

    def remote(source, target, send, recv, peer):
        return pltpu.make_async_remote_copy(
            src_ref=source, dst_ref=target, send_sem=send, recv_sem=recv,
            device_id={"ctx": peer}, device_id_type=MESH,
        )

    def outward(side):
        return after if side == 0 else before

    def inward(side):
        return before if side == 0 else after

    def q_copy(w, side, d, h):
        source = 0 if d == 1 else slot(side, d - 1)
        return remote(
            qt.at[w, source, h], qt.at[w, slot(side, d), h],
            q_send.at[w, side, d - 1, h], q_recv.at[w, side, d - 1, h], outward(side),
        )

    def t_copy(side, d):
        source = 0 if d == 1 else slot(side, d - 1) if d <= NEAR + 1 else FAR7[side]
        target = slot(side, d) if d <= NEAR else FAR7[side] if d == NEAR + 1 else FAR8
        return remote(tab.at[source], tab.at[target], t_send.at[side, d - 1], t_recv.at[side, d - 1], outward(side))

    def sel7_copy(w, side):
        return remote(
            sel7.at[w, side], qt.at[w, FAR7[side], 0],
            q_send.at[w, side, 6, 0], q_recv.at[w, side, 6, 0], outward(side),
        )

    def sel8_copy(w, side):
        return remote(
            sel8.at[w, side], pass8.at[w, side], q_send.at[w, side, 6, 1], q_recv.at[w, side, 6, 1], outward(side)
        )

    def pass8_copy(w, side):
        return remote(
            pass8.at[w, side],
            qt.at[w, FAR8, 0, pl.ds(side * half * LANES, half * LANES)],
            q_send.at[w, side, 7, 0], q_recv.at[w, side, 7, 0], outward(side),
        )

    def far_copy(w, side, i, source, target):
        return remote(source, target, f_send.at[w, side, i], f_recv.at[w, side, i], inward(side))

    def far8_copies(w, side):
        return [
            far_copy(w, side, 0, od8.at[w, pl.ds(side * half, half)], a8.at[w, side]),
            far_copy(w, side, 1, plse.at[w, FAR8], a8l.at[w, side]),
        ]

    def far8_passes(w, side):
        return [
            far_copy(w, side, 2, a8.at[w, side], b8.at[w, side]),
            far_copy(w, side, 3, a8l.at[w, side], b8l.at[w, side]),
        ]

    def far7_copies(w, side):
        return [
            far_copy(w, side, 4, od7.at[w, side], b7.at[w, side]),
            far_copy(w, side, 5, plse.at[w, FAR7[side]], b7l.at[w, side]),
        ]

    def chain_copies(w, side, d, h):
        return [
            remote(
                ref.at[w, side, d, h], ref.at[w, side, d - 1, h],
                c_send.at[w, side, d - 1, h, i], c_recv.at[w, side, d - 1, h, i], inward(side),
            )
            for i, ref in enumerate((chain, clse))
        ]

    def chosen(u, index):
        found = jnp.sum(jnp.where(lane == index, tab[u], 0.0), axis=1, keepdims=True)
        return jnp.broadcast_to(found, (8, LANES))[0:1, :]

    def is_head(want, h):
        return jnp.where(want == float(h + 1), 1.0, 0.0)

    def columns(j):
        return pl.ds(j * LANES, LANES)

    table = jnp.zeros((8, LANES), F32)
    for h in range(2):
        for k in range(3):
            table = jnp.where(lane == picks[0, h, k], float(h + 1), table)
    tab[0] = table

    loads[0].wait()
    for h in range(2):
        for w in range(WAVES):
            qt[w, 0, h] = q_own[w * span:(w + 1) * span, columns(h)]
    pl.semaphore_wait(barrier, 2)
    for side in range(2):
        t_copy(side, 1).start()
    for w in range(WAVES):
        for h in range(2):
            for side in range(2):
                q_copy(w, side, 1, h).start()

    def build(w, u):
        want = chosen(u, z)
        several = jnp.where(u < FAR7[0], 1, 0)
        for h in range(2):
            qm[:, columns(h)] = qt[w, u, h * several] * is_head(want, h).astype(BF16)

    def score(c, i, s_ref, m_ref):
        s = matmul(qm[...], kt[c, :, i * PIECE:(i + 1) * PIECE])
        for r in range(0, span, STRIP):
            strip = s[r:r + STRIP]
            s_ref[c, r:r + STRIP, i * PIECE:(i + 1) * PIECE] = strip
            top = m_ref[r:r + STRIP, :]
            for j in range(0, PIECE, LANES):
                top = jnp.maximum(top, strip[:, j:j + LANES])
            m_ref[r:r + STRIP, :] = top

    def weigh(c, first, last, s_ref, m_ref):
        strips = []
        for r in range(first, last, STRIP):
            top = jnp.concatenate([m_ref[r:r + STRIP, :]] * (CHUNK // LANES), axis=1)
            strips.append(jnp.exp2((s_ref[c, r:r + STRIP, :] - top) * rate).astype(BF16))
        return strips

    def absorb(c, strips, keep):
        at = pl.ds(pl.multiple_of(c * CHUNK, CHUNK), CHUNK)
        vw[c, :, 0:LANES] = values[at, 0:LANES] * keep[0] + values[at, LANES:2 * LANES] * keep[1]
        acc[...] += matmul(jnp.concatenate(strips, axis=0), vw[c])

    def chunks(body):
        def several(i, _):
            for k in range(UNROLL):
                body(i * UNROLL + k)
            return 0

        lax.fori_loop(0, n_chunks // UNROLL, several, 0)

    def lowest(m_ref):
        m_ref[...] = jnp.full((span, LANES), NEG, F32)

    def spread(m_ref):
        m_ref[...] = jnp.broadcast_to(jnp.max(m_ref[...], axis=1, keepdims=True), (span, LANES))

    def keepers(u):
        want = chosen(u, z)
        return [is_head(want, h).astype(BF16) for h in range(2)]

    def finish(w, u, m_ref):
        across = lax.broadcasted_iota(jnp.int32, (LANES, LANES), 1)
        packed = jnp.zeros((LANES, LANES), F32)
        for j in range(blocks):
            cut = slice(j * LANES, (j + 1) * LANES)
            total = acc[cut, LANES:2 * LANES]
            part[w, u, j] = jnp.transpose(acc[cut, 0:LANES] * (1.0 / total))
            packed = jnp.where(across == 8 * j, m_ref[cut, :] * rate + jnp.log2(total), packed)
        packed = jnp.transpose(packed)
        for j in range(blocks):
            plse[w, u, j:j + 1, :] = packed[8 * j:8 * j + 1, :]

    def only_score(w, u, s_ref, m_ref):
        build(w, u)
        lowest(m_ref)

        def body(c):
            for i in range(CHUNK // PIECE):
                score(c, i, s_ref, m_ref)

        chunks(body)
        spread(m_ref)

    def phase(g, s_new, m_new, s_old, m_old):
        w, u = g // UNITS, lax.rem(g, UNITS)
        w_old, u_old = (g - 1) // UNITS, lax.rem(g - 1, UNITS)
        build(w, u)
        lowest(m_new)
        keep = keepers(u_old)
        acc[...] = jnp.zeros_like(acc)

        def body(c):
            strips = []
            parts = CHUNK // PIECE
            for i in range(parts):
                score(c, i, s_new, m_new)
                strips += weigh(c, i * span // parts, (i + 1) * span // parts, s_old, m_old)
            absorb(c, strips, keep)

        chunks(body)
        finish(w_old, u_old, m_old)
        spread(m_new)

    def only_weigh(w, u, s_old, m_old):
        keep = keepers(u)
        acc[...] = jnp.zeros_like(acc)
        chunks(lambda c: absorb(c, weigh(c, 0, span, s_old, m_old), keep))
        finish(w, u, m_old)

    def relay(w, d, h):
        for side in range(2):
            q_copy(w, side, d, h).wait_recv()
            if d < NEAR:
                q_copy(w, side, d + 1, h).start()
            if w == 0 and h == 0:
                t_copy(side, d).wait_recv()
                t_copy(side, d + 1).start()

    def wanted(side):
        u = slot(side, NEAR)
        step = 1 if side == 0 else ranks - 1
        return [chosen(u, lax.rem(z + i * step, ranks)) for i in range(3)]

    def narrow(w):
        for side in range(2):
            _, want7, want8 = wanted(side)
            first, second = (qt[w, slot(side, NEAR), h] for h in range(2))
            sel7[w, side] = first * is_head(want7, 0).astype(BF16) + second * is_head(want7, 1).astype(BF16)
            cut = slice(side * half * LANES, (side + 1) * half * LANES)
            sel8[w, side] = first[cut] * is_head(want8, 0).astype(BF16) + second[cut] * is_head(want8, 1).astype(BF16)
            sel8_copy(w, side).start()
            sel7_copy(w, side).start()

    def pass_on(w):
        for side in range(2):
            sel8_copy(w, side).wait_recv()
            pass8_copy(w, side).start()
        if w == 0:
            for side in range(2):
                t_copy(side, 7).wait_recv()
            t_copy(0, 8).start()
        for side in range(2):
            sel7_copy(w, side).wait_recv()

    def arrive(w):
        if w == 0:
            t_copy(0, 8).wait_recv()
        for side in range(2):
            pass8_copy(w, side).wait_recv()

    def give7(w, side):
        od7[w, side] = part[w, FAR7[side]].astype(BF16)
        for copy in far7_copies(w, side):
            copy.start()

    def give8(w):
        od8[w] = part[w, FAR8].astype(BF16)
        for side in range(2):
            for copy in far8_copies(w, side):
                copy.start()

    def pass_back(w):
        for side in range(2):
            for copy in far8_copies(w, side):
                copy.wait_recv()
            for copy in far8_passes(w, side):
                copy.start()

    def own_lse(want, h, w, u, j):
        return jnp.where(want == float(h + 1), plse[w, u, j:j + 1, :], NEG)

    def gather6(w, h):
        for side in range(2):
            if h == 0:
                for copy in far7_copies(w, side) + far8_passes(w, side):
                    copy.wait_recv()
            u = slot(side, NEAR)
            want6, want7, want8 = wanted(side)
            for j in range(blocks):
                o, lse = mix(
                    part[w, u, j], own_lse(want6, h, w, u, j),
                    b7[w, side, j].astype(F32), jnp.where(want7 == float(h + 1), b7l[w, side, j:j + 1, :], NEG),
                )
                if j // half == side:
                    o, lse = mix(
                        o, lse, b8[w, side, j % half].astype(F32),
                        jnp.where(want8 == float(h + 1), b8l[w, side, j:j + 1, :], NEG),
                    )
                chain[w, side, NEAR, h, j] = o.astype(BF16)
                clse[w, side, NEAR, h, j:j + 1, :] = lse
            for copy in chain_copies(w, side, NEAR, h):
                copy.start()

    def back(w, d, h):
        for side in range(2):
            for copy in chain_copies(w, side, d + 1, h):
                copy.wait_recv()
            u = slot(side, d)
            want = chosen(u, z)
            for j in range(blocks):
                o, lse = mix(
                    chain[w, side, d, h, j].astype(F32), clse[w, side, d, h, j:j + 1, :],
                    part[w, u, j], own_lse(want, h, w, u, j),
                )
                chain[w, side, d, h, j] = o.astype(BF16)
                clse[w, side, d, h, j:j + 1, :] = lse
            for copy in chain_copies(w, side, d, h):
                copy.start()

    def final(w, h):
        for side in range(2):
            for copy in chain_copies(w, side, 1, h):
                copy.wait_recv()
        for j in range(blocks):
            at = w * blocks + j
            o, lse = mine[h, at], mlse[h, at:at + 1, :]
            for side in range(2):
                o, lse = mix(o, lse, chain[w, side, 0, h, j].astype(F32), clse[w, side, 0, h, j:j + 1, :])
            out[columns(at), columns(h)] = jnp.transpose(o).astype(BF16)

    def causal(h):
        key_at = lax.broadcasted_iota(jnp.int32, (rows, span), 0)
        query_at = lax.broadcasted_iota(jnp.int32, (rows, span), 1)
        vt_own[h] = flipped(v_own[:, columns(h)])
        want = chosen(0, z)
        for w in range(WAVES):
            s = jnp.where(key_at <= query_at + w * span, against(k_own[:, columns(h)], qt[w, 0, h]), NEG)
            top = jnp.max(fold(s, jnp.max), axis=0, keepdims=True)
            p = jnp.exp2((s - top) * rate)
            total = jnp.sum(fold(p, jnp.sum), axis=0, keepdims=True)
            o = matmul(vt_own[h], p.astype(BF16)) * (1.0 / total)
            lse = top * rate + jnp.log2(total)
            for j in range(blocks):
                cut = slice(j * LANES, (j + 1) * LANES)
                at = w * blocks + j
                mixed, both = mix(o[:, cut], lse[:, cut], part[w, 0, j], own_lse(want, h, w, 0, j))
                mine[h, at] = mixed
                mlse[h, at:at + 1, :] = both

    steps = {}

    def place(g, step, *args):
        steps.setdefault(g, []).append(functools.partial(step, *args))

    for d in range(2, NEAR + 1):
        for h in range(2):
            place(2 * d - 3 + h, relay, 0, d, h)
    place(2 * NEAR - 2, narrow, 0)
    place(13, pass_on, 0)
    place(14, arrive, 0)
    place(15, give7, 0, 0)

    def run(g):
        for k in sorted(steps):
            if k % 2 == g[1]:

                @pl.when(g[0] == k)
                def _(k=k):
                    for step in steps[k]:
                        step()

    for c in range(n_chunks):
        vw[c, :, LANES:2 * LANES] = jnp.ones((CHUNK, LANES), BF16)
    loads[1].wait()
    for c in range(n_chunks):
        kt[c] = flipped(keys[c * CHUNK:(c + 1) * CHUNK, :])
    only_score(0, 0, s_a, m_a)
    loads[2].wait()
    for h in range(2):
        relay(0, 1, h)

    def pair(i, _):
        run((2 * i - 1, 1))
        phase(2 * i - 1, s_b, m_b, s_a, m_a)
        run((2 * i, 0))
        phase(2 * i, s_a, m_a, s_b, m_b)
        return 0

    last = WAVES * UNITS - 1
    lax.fori_loop(1, (last + 1) // 2, pair, 0)
    for step in steps[last]:
        step()
    phase(last, s_b, m_b, s_a, m_a)
    give8(0)
    only_weigh(0, UNITS - 1, s_b, m_b)
    give7(0, 1)
    pass_back(0)
    for load in loads[3:]:
        load.wait()
    for h in range(2):
        causal(h)
    for h in range(2):
        gather6(0, h)
    for d in range(NEAR - 1, 0, -1):
        for h in range(2):
            back(0, d, h)
    for h in range(2):
        final(0, h)

    for side in range(2):
        for d in range(1, NEAR + 2):
            t_copy(side, d).wait_send()
    t_copy(0, 8).wait_send()
    for w in range(WAVES):
        for side in range(2):
            for h in range(2):
                for d in range(1, NEAR + 1):
                    q_copy(w, side, d, h).wait_send()
                    for copy in chain_copies(w, side, d, h):
                        copy.wait_send()
            for copy in [sel7_copy(w, side), sel8_copy(w, side), pass8_copy(w, side)]:
                copy.wait_send()
            for copy in far8_copies(w, side) + far8_passes(w, side) + far7_copies(w, side):
                copy.wait_send()


def shards(queries, keys_own, values_own, keys_cache, values_cache, picks):
    ranks = lax.axis_size("ctx")
    rows, width = queries.shape
    depth = keys_cache.shape[0]
    span = rows // WAVES
    blocks = span // LANES
    half = blocks // 2
    rate = (width // 2) ** (-0.5) * math.log2(math.e)
    return pl.pallas_call(
        functools.partial(kernel, ranks, rate),
        out_shape=jax.ShapeDtypeStruct((rows, width), BF16),
        in_specs=[pl.BlockSpec(memory_space=pltpu.SMEM)] + [pl.BlockSpec(memory_space=pl.ANY)] * 5,
        out_specs=pl.BlockSpec(memory_space=pltpu.VMEM),
        scratch_shapes=[
            pltpu.VMEM((rows, width), BF16),
            pltpu.VMEM((rows, width), BF16),
            pltpu.VMEM((rows, width), BF16),
            pltpu.VMEM((2, LANES, rows), BF16),
            pltpu.VMEM((depth, width), BF16),
            pltpu.VMEM((depth, width), BF16),
            pltpu.VMEM((depth // CHUNK, width, CHUNK), BF16),
            pltpu.VMEM((depth // CHUNK, CHUNK, width), BF16),
            pltpu.VMEM((WAVES, UNITS, 2, span, LANES), BF16),
            pltpu.VMEM((UNITS, 8, LANES), F32),
            pltpu.VMEM((span, width), BF16),
            pltpu.VMEM((depth // CHUNK, span, CHUNK), F32),
            pltpu.VMEM((depth // CHUNK, span, CHUNK), F32),
            pltpu.VMEM((span, LANES), F32),
            pltpu.VMEM((span, LANES), F32),
            pltpu.VMEM((span, width), F32),
            pltpu.VMEM((WAVES, UNITS, blocks, LANES, LANES), F32),
            pltpu.VMEM((WAVES, UNITS, blocks, LANES), F32),
            pltpu.VMEM((2, WAVES * blocks, LANES, LANES), F32),
            pltpu.VMEM((2, WAVES * blocks, LANES), F32),
            pltpu.VMEM((WAVES, 2, span, LANES), BF16),
            pltpu.VMEM((WAVES, 2, span // 2, LANES), BF16),
            pltpu.VMEM((WAVES, 2, span // 2, LANES), BF16),
            pltpu.VMEM((WAVES, blocks, LANES, LANES), BF16),
            pltpu.VMEM((WAVES, 2, blocks, LANES, LANES), BF16),
            pltpu.VMEM((WAVES, 2, half, LANES, LANES), BF16),
            pltpu.VMEM((WAVES, 2, blocks, LANES), F32),
            pltpu.VMEM((WAVES, 2, half, LANES, LANES), BF16),
            pltpu.VMEM((WAVES, 2, blocks, LANES), F32),
            pltpu.VMEM((WAVES, 2, blocks, LANES, LANES), BF16),
            pltpu.VMEM((WAVES, 2, blocks, LANES), F32),
            pltpu.VMEM((WAVES, 2, NEAR + 1, 2, blocks, LANES, LANES), BF16),
            pltpu.VMEM((WAVES, 2, NEAR + 1, 2, blocks, LANES), F32),
            pltpu.SemaphoreType.DMA((5,)),
            pltpu.SemaphoreType.DMA((WAVES, 2, 8, 2)),
            pltpu.SemaphoreType.DMA((WAVES, 2, 8, 2)),
            pltpu.SemaphoreType.DMA((2, 8)),
            pltpu.SemaphoreType.DMA((2, 8)),
            pltpu.SemaphoreType.DMA((WAVES, 2, 6)),
            pltpu.SemaphoreType.DMA((WAVES, 2, 6)),
            pltpu.SemaphoreType.DMA((WAVES, 2, NEAR, 2, 2)),
            pltpu.SemaphoreType.DMA((WAVES, 2, NEAR, 2, 2)),
        ],
        compiler_params=pltpu.CompilerParams(
            collective_id=0, has_side_effects=True, vmem_limit_bytes=56 * 1024 * 1024
        ),
        cost_estimate=pl.CostEstimate(
            flops=4 * 16 * depth * rows * width, bytes_accessed=2 * (2 * depth + 4 * rows) * width,
            transcendentals=16 * depth * rows,
        ),
    )(picks, queries, keys_own, values_own, keys_cache, values_cache)


def solution(mesh):
    placed = P(("req", "ctx"), "head")
    return jax.shard_map(
        shards,
        mesh=mesh,
        in_specs=(placed,) * 5 + (P(("req", "ctx"), "head", None),),
        out_specs=placed,
        check_vma=False,
    )
```

```python
import functools
import math

import jax
import jax.numpy as jnp
from jax import lax
from jax.experimental import pallas as pl
from jax.experimental.pallas import tpu as pltpu
from jax.sharding import PartitionSpec as P

NEG = -1e30
LANES = 128
CHUNK = 1024
PIECE = 512
STRIP = 64
UNROLL = 2
NEAR = 6
FAR8 = 13
FAR7 = (14, 15)
WAVES = 1
UNITS = 2 * NEAR + 4
MESH = pl.DeviceIdType.MESH
F32 = jnp.float32
BF16 = jnp.bfloat16


def matmul(a, b):
    return lax.dot_general(a, b, (((1,), (0,)), ((), ())), preferred_element_type=F32)


def against(a, b):
    return lax.dot_general(a, b, (((1,), (1,)), ((), ())), preferred_element_type=F32)


def flipped(x):
    width = x.shape[1]
    rows = lax.broadcasted_iota(jnp.int32, (width, width), 0)
    columns = lax.broadcasted_iota(jnp.int32, (width, width), 1)
    eye = jnp.where(rows == columns, 1.0, 0.0).astype(BF16)
    return against(eye, x).astype(BF16)


def fold(x, op):
    return op(x.reshape(x.shape[0] // 8, 8, x.shape[1]), axis=0)


def mix(o1, l1, o2, l2):
    best = jnp.maximum(l1, l2)
    a = jnp.exp2(l1 - best)
    b = jnp.exp2(l2 - best)
    total = a + b
    part = 1.0 / total
    return o1 * (a * part) + o2 * (b * part), best + jnp.log2(total)


def slot(side, d):
    return 2 * d - 1 + side


def kernel(
    ranks, rate,
    picks, q_in, ko_in, vo_in, k_in, v_in,
    out,
    q_own, k_own, v_own, vt_own, keys, values, kt, vw,
    qt, tab, qm, s_a, s_b, m_a, m_b, acc,
    part, plse, mine, mlse,
    sel7, sel8, pass8,
    od8, od7, a8, a8l, b8, b8l, b7, b7l, chain, clse,
    load_sem, q_send, q_recv, t_send, t_recv, f_send, f_recv, c_send, c_recv,
):
    z = lax.axis_index("ctx")
    after = lax.rem(z + 1, ranks)
    before = lax.rem(z + ranks - 1, ranks)
    rows = q_own.shape[0]
    span = rows // WAVES
    blocks = span // LANES
    half = blocks // 2
    n_chunks = keys.shape[0] // CHUNK
    lane = lax.broadcasted_iota(jnp.int32, (8, LANES), 1)

    loads = [
        pltpu.make_async_copy(source, target, load_sem.at[i])
        for i, (source, target) in enumerate(
            [(q_in, q_own), (k_in, keys), (v_in, values), (ko_in, k_own), (vo_in, v_own)]
        )
    ]
    for load in loads:
        load.start()

    barrier = pltpu.get_barrier_semaphore()
    for peer in (before, after):
        pl.semaphore_signal(barrier, inc=1, device_id={"ctx": peer}, device_id_type=MESH)

    def remote(source, target, send, recv, peer):
        return pltpu.make_async_remote_copy(
            src_ref=source, dst_ref=target, send_sem=send, recv_sem=recv,
            device_id={"ctx": peer}, device_id_type=MESH,
        )

    def outward(side):
        return after if side == 0 else before

    def inward(side):
        return before if side == 0 else after

    def cut(r):
        return pl.ds(r * half * LANES, half * LANES)

    def q_copy(w, side, d, h, r):
        source = 0 if d == 1 else slot(side, d - 1)
        return remote(
            qt.at[w, source, h, cut(r)], qt.at[w, slot(side, d), h, cut(r)],
            q_send.at[w, side, d - 1, h, r], q_recv.at[w, side, d - 1, h, r], outward(side),
        )

    def t_copy(side, d):
        source = 0 if d == 1 else slot(side, d - 1) if d <= NEAR + 1 else FAR7[side]
        target = slot(side, d) if d <= NEAR else FAR7[side] if d == NEAR + 1 else FAR8
        return remote(tab.at[source], tab.at[target], t_send.at[side, d - 1], t_recv.at[side, d - 1], outward(side))

    def sel7_copy(w, side, r):
        return remote(
            sel7.at[w, side, cut(r)], qt.at[w, FAR7[side], 0, cut(r)],
            q_send.at[w, side, 6, 0, r], q_recv.at[w, side, 6, 0, r], outward(side),
        )

    def sel8_copy(w, side):
        return remote(
            sel8.at[w, side], pass8.at[w, side], q_send.at[w, side, 6, 1, 0], q_recv.at[w, side, 6, 1, 0], outward(side)
        )

    def pass8_copy(w, side):
        return remote(
            pass8.at[w, side],
            qt.at[w, FAR8, 0, cut(side)],
            q_send.at[w, side, 7, 0, 0], q_recv.at[w, side, 7, 0, 0], outward(side),
        )

    def far_copy(w, side, i, source, target):
        return remote(source, target, f_send.at[w, side, i], f_recv.at[w, side, i], inward(side))

    def far8_copies(w, side):
        return [
            far_copy(w, side, 0, od8.at[w, pl.ds(side * half, half)], a8.at[w, side]),
            far_copy(w, side, 1, plse.at[w, FAR8], a8l.at[w, side]),
        ]

    def far8_passes(w, side):
        return [
            far_copy(w, side, 2, a8.at[w, side], b8.at[w, side]),
            far_copy(w, side, 3, a8l.at[w, side], b8l.at[w, side]),
        ]

    def far7_copies(w, side):
        return [
            far_copy(w, side, 4, od7.at[w, side], b7.at[w, side]),
            far_copy(w, side, 5, plse.at[w, FAR7[side]], b7l.at[w, side]),
        ]

    def chain_copies(w, side, d, h, r):
        return [
            remote(
                ref.at[w, side, d, h, r], ref.at[w, side, d - 1, h, r],
                c_send.at[w, side, d - 1, h, r, i], c_recv.at[w, side, d - 1, h, r, i], inward(side),
            )
            for i, ref in enumerate((chain, clse))
        ]

    def chosen(u, index):
        found = jnp.sum(jnp.where(lane == index, tab[u], 0.0), axis=1, keepdims=True)
        return jnp.broadcast_to(found, (8, LANES))[0:1, :]

    def is_head(want, h):
        return jnp.where(want == float(h + 1), 1.0, 0.0)

    def columns(j):
        return pl.ds(j * LANES, LANES)

    table = jnp.zeros((8, LANES), F32)
    for h in range(2):
        for k in range(3):
            table = jnp.where(lane == picks[0, h, k], float(h + 1), table)
    tab[0] = table

    loads[0].wait()
    for h in range(2):
        for w in range(WAVES):
            qt[w, 0, h] = q_own[w * span:(w + 1) * span, columns(h)]
    pl.semaphore_wait(barrier, 2)
    for side in range(2):
        t_copy(side, 1).start()
    for i in range(4):
        for side in range(2):
            q_copy(0, side, 1, i % 2, (i // 2) ^ side).start()

    def build(w, u):
        want = chosen(u, z)
        several = jnp.where(u < FAR8, 1, 0)
        for h in range(2):
            qm[:, columns(h)] = qt[w, u, h * several] * is_head(want, h).astype(BF16)

    def score(c, i, s_ref, m_ref):
        s = matmul(qm[...], kt[c, :, i * PIECE:(i + 1) * PIECE])
        for r in range(0, span, STRIP):
            strip = s[r:r + STRIP]
            s_ref[c, r:r + STRIP, i * PIECE:(i + 1) * PIECE] = strip
            top = m_ref[r:r + STRIP, :]
            for j in range(0, PIECE, LANES):
                top = jnp.maximum(top, strip[:, j:j + LANES])
            m_ref[r:r + STRIP, :] = top

    def weigh(c, first, last, s_ref, m_ref):
        strips = []
        for r in range(first, last, STRIP):
            top = jnp.concatenate([m_ref[r:r + STRIP, :]] * (CHUNK // LANES), axis=1)
            strips.append(jnp.exp2((s_ref[c, r:r + STRIP, :] - top) * rate).astype(BF16))
        return strips

    def absorb(c, strips, keep):
        at = pl.ds(pl.multiple_of(c * CHUNK, CHUNK), CHUNK)
        vw[c, :, 0:LANES] = values[at, 0:LANES] * keep[0] + values[at, LANES:2 * LANES] * keep[1]
        acc[...] += matmul(jnp.concatenate(strips, axis=0), vw[c])

    def chunks(body, middle=None):
        def several(i, _):
            if middle is not None:
                pl.when(i == 1)(middle)
            for k in range(UNROLL):
                body(i * UNROLL + k)
            return 0

        lax.fori_loop(0, n_chunks // UNROLL, several, 0)

    def lowest(m_ref):
        m_ref[...] = jnp.full((span, LANES), NEG, F32)

    def spread(m_ref):
        m_ref[...] = jnp.broadcast_to(jnp.max(m_ref[...], axis=1, keepdims=True), (span, LANES))

    def keepers(u):
        want = chosen(u, z)
        return [is_head(want, h).astype(BF16) for h in range(2)]

    def finish(w, u, m_ref):
        across = lax.broadcasted_iota(jnp.int32, (LANES, LANES), 1)
        packed = jnp.zeros((LANES, LANES), F32)
        for j in range(blocks):
            cut = slice(j * LANES, (j + 1) * LANES)
            total = acc[cut, LANES:2 * LANES]
            part[w, u, j] = jnp.transpose(acc[cut, 0:LANES] * (1.0 / total))
            packed = jnp.where(across == 8 * j, m_ref[cut, :] * rate + jnp.log2(total), packed)
        packed = jnp.transpose(packed)
        for j in range(blocks):
            plse[w, u, j:j + 1, :] = packed[8 * j:8 * j + 1, :]

    def only_score(w, u, s_ref, m_ref):
        build(w, u)
        lowest(m_ref)

        def body(c):
            for i in range(CHUNK // PIECE):
                score(c, i, s_ref, m_ref)

        chunks(body)
        spread(m_ref)

    def phase(g, parity, s_new, m_new, s_old, m_old):
        w, u = g // UNITS, lax.rem(g, UNITS)
        w_old, u_old = (g - 1) // UNITS, lax.rem(g - 1, UNITS)
        build(w, u)
        lowest(m_new)
        keep = keepers(u_old)
        acc[...] = jnp.zeros_like(acc)

        def body(c):
            strips = []
            parts = CHUNK // PIECE
            for i in range(parts):
                score(c, i, s_new, m_new)
                strips += weigh(c, i * span // parts, (i + 1) * span // parts, s_old, m_old)
            absorb(c, strips, keep)

        chunks(body, functools.partial(run, g, parity, 1))
        finish(w_old, u_old, m_old)
        spread(m_new)

    def only_weigh(w, u, s_old, m_old):
        keep = keepers(u)
        acc[...] = jnp.zeros_like(acc)
        chunks(lambda c: absorb(c, weigh(c, 0, span, s_old, m_old), keep))
        finish(w, u, m_old)

    def relay(w, d, i):
        for side in range(2):
            h, r = i % 2, (i // 2) ^ side
            q_copy(w, side, d, h, r).wait_recv()
            if d < NEAR:
                q_copy(w, side, d + 1, h, r).start()
            if i == 0:
                t_copy(side, d).wait_recv()
                t_copy(side, d + 1).start()

    def wanted(side):
        u = slot(side, NEAR)
        step = 1 if side == 0 else ranks - 1
        return [chosen(u, lax.rem(z + i * step, ranks)) for i in range(3)]

    def narrow(w, i):
        for side in range(2):
            _, want7, want8 = wanted(side)
            r = i ^ side
            rows_of = slice(r * half * LANES, (r + 1) * half * LANES)
            first, second = (qt[w, slot(side, NEAR), h, rows_of] for h in range(2))
            if i == 0:
                sel8[w, side] = first * is_head(want8, 0).astype(BF16) + second * is_head(want8, 1).astype(BF16)
                sel8_copy(w, side).start()
            sel7[w, side, rows_of] = first * is_head(want7, 0).astype(BF16) + second * is_head(want7, 1).astype(BF16)
            sel7_copy(w, side, r).start()

    def pass_on(w):
        for side in range(2):
            sel8_copy(w, side).wait_recv()
            pass8_copy(w, side).start()
        for side in range(2):
            t_copy(side, 7).wait_recv()
        t_copy(0, 8).start()

    def arrive8(w):
        t_copy(0, 8).wait_recv()
        for side in range(2):
            pass8_copy(w, side).wait_recv()

    def arrive7(w, side):
        for r in range(2):
            sel7_copy(w, side, r).wait_recv()

    def give7(w, side):
        od7[w, side] = part[w, FAR7[side]].astype(BF16)
        for copy in far7_copies(w, side):
            copy.start()

    def give8(w):
        od8[w] = part[w, FAR8].astype(BF16)
        for side in range(2):
            for copy in far8_copies(w, side):
                copy.start()

    def pass_back(w):
        for side in range(2):
            for copy in far8_copies(w, side):
                copy.wait_recv()
            for copy in far8_passes(w, side):
                copy.start()

    def own_lse(want, h, w, u, j):
        return jnp.where(want == float(h + 1), plse[w, u, j:j + 1, :], NEG)

    def gather6(w, side):
        for copy in far7_copies(w, side) + far8_passes(w, side):
            copy.wait_recv()
        u = slot(side, NEAR)
        want6, want7, want8 = wanted(side)
        for r in range(2):
            for h in range(2):
                for k in range(half):
                    j = r * half + k
                    o, lse = mix(
                        part[w, u, j], own_lse(want6, h, w, u, j),
                        b7[w, side, j].astype(F32), jnp.where(want7 == float(h + 1), b7l[w, side, j:j + 1, :], NEG),
                    )
                    if r == side:
                        o, lse = mix(
                            o, lse, b8[w, side, k].astype(F32),
                            jnp.where(want8 == float(h + 1), b8l[w, side, j:j + 1, :], NEG),
                        )
                    chain[w, side, NEAR, h, r, k] = o.astype(BF16)
                    clse[w, side, NEAR, h, r, k:k + 1, :] = lse
                for copy in chain_copies(w, side, NEAR, h, r):
                    copy.start()

    def back(w, d, h, r):
        for side in range(2):
            for copy in chain_copies(w, side, d + 1, h, r):
                copy.wait_recv()
            u = slot(side, d)
            want = chosen(u, z)
            for k in range(half):
                o, lse = mix(
                    chain[w, side, d, h, r, k].astype(F32), clse[w, side, d, h, r, k:k + 1, :],
                    part[w, u, r * half + k], own_lse(want, h, w, u, r * half + k),
                )
                chain[w, side, d, h, r, k] = o.astype(BF16)
                clse[w, side, d, h, r, k:k + 1, :] = lse
            for copy in chain_copies(w, side, d, h, r):
                copy.start()

    def final(w, h, r):
        for side in range(2):
            for copy in chain_copies(w, side, 1, h, r):
                copy.wait_recv()
        for k in range(half):
            at = w * blocks + r * half + k
            o, lse = mine[h, at], mlse[h, at:at + 1, :]
            for side in range(2):
                o, lse = mix(o, lse, chain[w, side, 0, h, r, k].astype(F32), clse[w, side, 0, h, r, k:k + 1, :])
            out[columns(at), columns(h)] = jnp.transpose(o).astype(BF16)

    def causal(h):
        key_at = lax.broadcasted_iota(jnp.int32, (rows, span), 0)
        query_at = lax.broadcasted_iota(jnp.int32, (rows, span), 1)
        vt_own[h] = flipped(v_own[:, columns(h)])
        want = chosen(0, z)
        for w in range(WAVES):
            s = jnp.where(key_at <= query_at + w * span, against(k_own[:, columns(h)], qt[w, 0, h]), NEG)
            top = jnp.max(fold(s, jnp.max), axis=0, keepdims=True)
            p = jnp.exp2((s - top) * rate)
            total = jnp.sum(fold(p, jnp.sum), axis=0, keepdims=True)
            o = matmul(vt_own[h], p.astype(BF16)) * (1.0 / total)
            lse = top * rate + jnp.log2(total)
            for j in range(blocks):
                cut = slice(j * LANES, (j + 1) * LANES)
                at = w * blocks + j
                mixed, both = mix(o[:, cut], lse[:, cut], part[w, 0, j], own_lse(want, h, w, 0, j))
                mine[h, at] = mixed
                mlse[h, at:at + 1, :] = both

    steps = {}

    def place(g, step, *args):
        steps.setdefault(g, []).append(functools.partial(step, *args))

    for d in range(2, NEAR + 1):
        for i in range(4):
            place(2 * (2 * d - 3) + i, relay, 0, d, i)
    place(2 * (2 * NEAR - 3) + 1, narrow, 0, 0)
    place(2 * (2 * NEAR - 3) + 3, narrow, 0, 1)
    place(2 * 11 + 1, pass_on, 0)
    place(2 * FAR8, arrive8, 0)
    place(2 * FAR7[0], arrive7, 0, 0)
    place(2 * FAR7[1], arrive7, 0, 1)
    place(2 * FAR7[1], give8, 0)

    def run(g, parity, middle):
        for k in sorted(steps):
            if k % 2 == middle and (k // 2) % 2 == parity:

                @pl.when(g == k // 2)
                def _(k=k):
                    for step in steps[k]:
                        step()

    for c in range(n_chunks):
        vw[c, :, LANES:2 * LANES] = jnp.ones((CHUNK, LANES), BF16)
    loads[1].wait()
    for c in range(n_chunks):
        kt[c] = flipped(keys[c * CHUNK:(c + 1) * CHUNK, :])
    only_score(0, 0, s_a, m_a)
    loads[2].wait()
    for i in range(4):
        relay(0, 1, i)

    def pair(i, _):
        run(2 * i - 1, 1, 0)
        phase(2 * i - 1, 1, s_b, m_b, s_a, m_a)
        run(2 * i, 0, 0)
        phase(2 * i, 0, s_a, m_a, s_b, m_b)
        return 0

    lax.fori_loop(1, UNITS // 2, pair, 0)
    for step in steps[2 * (UNITS - 1)]:
        step()
    phase(UNITS - 1, 1, s_b, m_b, s_a, m_a)
    give7(0, 0)
    pass_back(0)
    only_weigh(0, UNITS - 1, s_b, m_b)
    give7(0, 1)
    for load in loads[3:]:
        load.wait()
    for side in range(2):
        gather6(0, side)
    for h in range(2):
        causal(h)
    order = [(h, r) for r in range(2) for h in range(2)]
    for d in range(NEAR - 1, 0, -1):
        for h, r in order:
            back(0, d, h, r)
    for h, r in order:
        final(0, h, r)

    for side in range(2):
        for d in range(1, NEAR + 2):
            t_copy(side, d).wait_send()
    t_copy(0, 8).wait_send()
    for w in range(WAVES):
        for side in range(2):
            for h in range(2):
                for r in range(2):
                    for d in range(1, NEAR + 1):
                        q_copy(w, side, d, h, r).wait_send()
                        for copy in chain_copies(w, side, d, h, r):
                            copy.wait_send()
            for copy in [sel7_copy(w, side, r) for r in range(2)] + [sel8_copy(w, side), pass8_copy(w, side)]:
                copy.wait_send()
            for copy in far8_copies(w, side) + far8_passes(w, side) + far7_copies(w, side):
                copy.wait_send()


def shards(queries, keys_own, values_own, keys_cache, values_cache, picks):
    ranks = lax.axis_size("ctx")
    rows, width = queries.shape
    depth = keys_cache.shape[0]
    span = rows // WAVES
    blocks = span // LANES
    half = blocks // 2
    rate = (width // 2) ** (-0.5) * math.log2(math.e)
    return pl.pallas_call(
        functools.partial(kernel, ranks, rate),
        out_shape=jax.ShapeDtypeStruct((rows, width), BF16),
        in_specs=[pl.BlockSpec(memory_space=pltpu.SMEM)] + [pl.BlockSpec(memory_space=pl.ANY)] * 5,
        out_specs=pl.BlockSpec(memory_space=pltpu.VMEM),
        scratch_shapes=[
            pltpu.VMEM((rows, width), BF16),
            pltpu.VMEM((rows, width), BF16),
            pltpu.VMEM((rows, width), BF16),
            pltpu.VMEM((2, LANES, rows), BF16),
            pltpu.VMEM((depth, width), BF16),
            pltpu.VMEM((depth, width), BF16),
            pltpu.VMEM((depth // CHUNK, width, CHUNK), BF16),
            pltpu.VMEM((depth // CHUNK, CHUNK, width), BF16),
            pltpu.VMEM((WAVES, UNITS, 2, span, LANES), BF16),
            pltpu.VMEM((UNITS, 8, LANES), F32),
            pltpu.VMEM((span, width), BF16),
            pltpu.VMEM((depth // CHUNK, span, CHUNK), F32),
            pltpu.VMEM((depth // CHUNK, span, CHUNK), F32),
            pltpu.VMEM((span, LANES), F32),
            pltpu.VMEM((span, LANES), F32),
            pltpu.VMEM((span, width), F32),
            pltpu.VMEM((WAVES, UNITS, blocks, LANES, LANES), F32),
            pltpu.VMEM((WAVES, UNITS, blocks, LANES), F32),
            pltpu.VMEM((2, WAVES * blocks, LANES, LANES), F32),
            pltpu.VMEM((2, WAVES * blocks, LANES), F32),
            pltpu.VMEM((WAVES, 2, span, LANES), BF16),
            pltpu.VMEM((WAVES, 2, span // 2, LANES), BF16),
            pltpu.VMEM((WAVES, 2, span // 2, LANES), BF16),
            pltpu.VMEM((WAVES, blocks, LANES, LANES), BF16),
            pltpu.VMEM((WAVES, 2, blocks, LANES, LANES), BF16),
            pltpu.VMEM((WAVES, 2, half, LANES, LANES), BF16),
            pltpu.VMEM((WAVES, 2, blocks, LANES), F32),
            pltpu.VMEM((WAVES, 2, half, LANES, LANES), BF16),
            pltpu.VMEM((WAVES, 2, blocks, LANES), F32),
            pltpu.VMEM((WAVES, 2, blocks, LANES, LANES), BF16),
            pltpu.VMEM((WAVES, 2, blocks, LANES), F32),
            pltpu.VMEM((WAVES, 2, NEAR + 1, 2, 2, half, LANES, LANES), BF16),
            pltpu.VMEM((WAVES, 2, NEAR + 1, 2, 2, half, LANES), F32),
            pltpu.SemaphoreType.DMA((5,)),
            pltpu.SemaphoreType.DMA((WAVES, 2, 8, 2, 2)),
            pltpu.SemaphoreType.DMA((WAVES, 2, 8, 2, 2)),
            pltpu.SemaphoreType.DMA((2, 8)),
            pltpu.SemaphoreType.DMA((2, 8)),
            pltpu.SemaphoreType.DMA((WAVES, 2, 6)),
            pltpu.SemaphoreType.DMA((WAVES, 2, 6)),
            pltpu.SemaphoreType.DMA((WAVES, 2, NEAR, 2, 2, 2)),
            pltpu.SemaphoreType.DMA((WAVES, 2, NEAR, 2, 2, 2)),
        ],
        compiler_params=pltpu.CompilerParams(
            collective_id=0, has_side_effects=True, vmem_limit_bytes=56 * 1024 * 1024
        ),
        cost_estimate=pl.CostEstimate(
            flops=4 * 16 * depth * rows * width, bytes_accessed=2 * (2 * depth + 4 * rows) * width,
            transcendentals=16 * depth * rows,
        ),
    )(picks, queries, keys_own, values_own, keys_cache, values_cache)


def solution(mesh):
    placed = P(("req", "ctx"), "head")
    return jax.shard_map(
        shards,
        mesh=mesh,
        in_specs=(placed,) * 5 + (P(("req", "ctx"), "head", None),),
        out_specs=placed,
        check_vma=False,
    )
```

```python
import functools
import math

import jax
import jax.numpy as jnp
from jax import lax
from jax.experimental import pallas as pl
from jax.experimental.pallas import tpu as pltpu
from jax.sharding import PartitionSpec as P

NEG = -1e30
LANES = 128
CHUNK = 1024
PIECE = 512
STRIP = 64
UNROLL = 2
NEAR = 6
FAR8 = 13
FAR7 = (14, 15)
WAVES = 1
UNITS = 2 * NEAR + 4
MESH = pl.DeviceIdType.MESH
F32 = jnp.float32
BF16 = jnp.bfloat16


def matmul(a, b):
    return lax.dot_general(a, b, (((1,), (0,)), ((), ())), preferred_element_type=F32)


def against(a, b):
    return lax.dot_general(a, b, (((1,), (1,)), ((), ())), preferred_element_type=F32)


def flipped(x):
    width = x.shape[1]
    rows = lax.broadcasted_iota(jnp.int32, (width, width), 0)
    columns = lax.broadcasted_iota(jnp.int32, (width, width), 1)
    eye = jnp.where(rows == columns, 1.0, 0.0).astype(BF16)
    return against(eye, x).astype(BF16)


def fold(x, op):
    return op(x.reshape(x.shape[0] // 8, 8, x.shape[1]), axis=0)


def mix(o1, l1, o2, l2):
    best = jnp.maximum(l1, l2)
    a = jnp.exp2(l1 - best)
    b = jnp.exp2(l2 - best)
    total = a + b
    part = 1.0 / total
    return o1 * (a * part) + o2 * (b * part), best + jnp.log2(total)


def slot(side, d):
    return 2 * d - 1 + side


def kernel(
    ranks, rate,
    picks, q_in, ko_in, vo_in, k_in, v_in,
    out,
    q_own, k_own, v_own, vt_own, keys, values, kt, vw,
    qt, tab, qm, s_a, s_b, m_a, m_b, acc,
    part, plse, mine, mlse,
    sel7, sel8, pass8,
    od8, od7, a8, a8l, b8, b8l, b7, b7l, chain, clse,
    load_sem, q_send, q_recv, t_send, t_recv, f_send, f_recv, c_send, c_recv,
):
    z = lax.axis_index("ctx")
    after = lax.rem(z + 1, ranks)
    before = lax.rem(z + ranks - 1, ranks)
    rows = q_own.shape[0]
    span = rows // WAVES
    blocks = span // LANES
    half = blocks // 2
    n_chunks = keys.shape[0] // CHUNK
    lane = lax.broadcasted_iota(jnp.int32, (8, LANES), 1)

    loads = [
        pltpu.make_async_copy(source, target, load_sem.at[i])
        for i, (source, target) in enumerate(
            [(q_in, q_own), (k_in, keys), (v_in, values), (ko_in, k_own), (vo_in, v_own)]
        )
    ]
    for load in loads:
        load.start()

    barrier = pltpu.get_barrier_semaphore()
    for peer in (before, after):
        pl.semaphore_signal(barrier, inc=1, device_id={"ctx": peer}, device_id_type=MESH)

    def remote(source, target, send, recv, peer):
        return pltpu.make_async_remote_copy(
            src_ref=source, dst_ref=target, send_sem=send, recv_sem=recv,
            device_id={"ctx": peer}, device_id_type=MESH,
        )

    def outward(side):
        return after if side == 0 else before

    def inward(side):
        return before if side == 0 else after

    def cut(r):
        return pl.ds(r * half * LANES, half * LANES)

    def q_copy(w, side, d, h, r):
        source = 0 if d == 1 else slot(side, d - 1)
        return remote(
            qt.at[w, source, h, cut(r)], qt.at[w, slot(side, d), h, cut(r)],
            q_send.at[w, side, d - 1, h, r], q_recv.at[w, side, d - 1, h, r], outward(side),
        )

    def t_copy(side, d):
        source = 0 if d == 1 else slot(side, d - 1) if d <= NEAR + 1 else FAR7[side]
        target = slot(side, d) if d <= NEAR else FAR7[side] if d == NEAR + 1 else FAR8
        return remote(tab.at[source], tab.at[target], t_send.at[side, d - 1], t_recv.at[side, d - 1], outward(side))

    def sel7_copy(w, side, r):
        return remote(
            sel7.at[w, side, cut(r)], qt.at[w, FAR7[side], 0, cut(r)],
            q_send.at[w, side, 6, 0, r], q_recv.at[w, side, 6, 0, r], outward(side),
        )

    def sel8_copy(w, side):
        return remote(
            sel8.at[w, side], pass8.at[w, side], q_send.at[w, side, 6, 1, 0], q_recv.at[w, side, 6, 1, 0], outward(side)
        )

    def pass8_copy(w, side):
        return remote(
            pass8.at[w, side],
            qt.at[w, FAR8, 0, cut(side)],
            q_send.at[w, side, 7, 0, 0], q_recv.at[w, side, 7, 0, 0], outward(side),
        )

    def far_copy(w, side, i, source, target):
        return remote(source, target, f_send.at[w, side, i], f_recv.at[w, side, i], inward(side))

    def far8_copies(w, side):
        return [
            far_copy(w, side, 0, od8.at[w, pl.ds(side * half, half)], a8.at[w, side]),
            far_copy(w, side, 1, plse.at[w, FAR8], a8l.at[w, side]),
        ]

    def far8_passes(w, side):
        return [
            far_copy(w, side, 2, a8.at[w, side], b8.at[w, side]),
            far_copy(w, side, 3, a8l.at[w, side], b8l.at[w, side]),
        ]

    def far7_copies(w, side):
        return [
            far_copy(w, side, 4, od7.at[w, side], b7.at[w, side]),
            far_copy(w, side, 5, plse.at[w, FAR7[side]], b7l.at[w, side]),
        ]

    def chain_copies(w, side, d, h, r):
        return [
            remote(
                ref.at[w, side, d, h, r], ref.at[w, side, d - 1, h, r],
                c_send.at[w, side, d - 1, h, r, i], c_recv.at[w, side, d - 1, h, r, i], inward(side),
            )
            for i, ref in enumerate((chain, clse))
        ]

    def chosen(u, index):
        found = jnp.sum(jnp.where(lane == index, tab[u], 0.0), axis=1, keepdims=True)
        return jnp.broadcast_to(found, (8, LANES))[0:1, :]

    def is_head(want, h):
        return jnp.where(want == float(h + 1), 1.0, 0.0)

    def columns(j):
        return pl.ds(j * LANES, LANES)

    table = jnp.zeros((8, LANES), F32)
    for h in range(2):
        for k in range(3):
            table = jnp.where(lane == picks[0, h, k], float(h + 1), table)
    tab[0] = table

    loads[0].wait()
    for h in range(2):
        for w in range(WAVES):
            qt[w, 0, h] = q_own[w * span:(w + 1) * span, columns(h)]
    pl.semaphore_wait(barrier, 2)
    for side in range(2):
        t_copy(side, 1).start()
    for i in range(4):
        for side in range(2):
            q_copy(0, side, 1, i % 2, (i // 2) ^ side).start()

    def build(w, u):
        want = chosen(u, z)
        several = jnp.where(u < FAR8, 1, 0)
        for h in range(2):
            qm[:, columns(h)] = qt[w, u, h * several] * is_head(want, h).astype(BF16)

    def score(c, i, s_ref, m_ref):
        s = matmul(qm[...], kt[c, :, i * PIECE:(i + 1) * PIECE])
        for r in range(0, span, STRIP):
            strip = s[r:r + STRIP]
            s_ref[c, r:r + STRIP, i * PIECE:(i + 1) * PIECE] = strip
            top = m_ref[r:r + STRIP, :]
            for j in range(0, PIECE, LANES):
                top = jnp.maximum(top, strip[:, j:j + LANES])
            m_ref[r:r + STRIP, :] = top

    def weigh(c, first, last, s_ref, m_ref):
        strips = []
        for r in range(first, last, STRIP):
            top = jnp.concatenate([m_ref[r:r + STRIP, :]] * (CHUNK // LANES), axis=1)
            strips.append(jnp.exp2((s_ref[c, r:r + STRIP, :] - top) * rate).astype(BF16))
        return strips

    def absorb(c, strips, keep):
        at = pl.ds(pl.multiple_of(c * CHUNK, CHUNK), CHUNK)
        vw[c, :, 0:LANES] = values[at, 0:LANES] * keep[0] + values[at, LANES:2 * LANES] * keep[1]
        acc[...] += matmul(jnp.concatenate(strips, axis=0), vw[c])

    def chunks(body, middle=None):
        def several(i, _):
            if middle is not None:
                pl.when(i == 1)(middle)
            for k in range(UNROLL):
                body(i * UNROLL + k)
            return 0

        lax.fori_loop(0, n_chunks // UNROLL, several, 0)

    def lowest(m_ref):
        m_ref[...] = jnp.full((span, LANES), NEG, F32)

    def spread(m_ref):
        m_ref[...] = jnp.broadcast_to(jnp.max(m_ref[...], axis=1, keepdims=True), (span, LANES))

    def keepers(u):
        want = chosen(u, z)
        return [is_head(want, h).astype(BF16) for h in range(2)]

    def finish(w, u, m_ref):
        across = lax.broadcasted_iota(jnp.int32, (LANES, LANES), 1)
        packed = jnp.zeros((LANES, LANES), F32)
        for j in range(blocks):
            cut = slice(j * LANES, (j + 1) * LANES)
            total = acc[cut, LANES:2 * LANES]
            part[w, u, j] = jnp.transpose(acc[cut, 0:LANES] * (1.0 / total))
            packed = jnp.where(across == 8 * j, m_ref[cut, :] * rate + jnp.log2(total), packed)
        packed = jnp.transpose(packed)
        for j in range(blocks):
            plse[w, u, j:j + 1, :] = packed[8 * j:8 * j + 1, :]

    def only_score(w, u, s_ref, m_ref):
        build(w, u)
        lowest(m_ref)

        def body(c):
            for i in range(CHUNK // PIECE):
                score(c, i, s_ref, m_ref)

        chunks(body)
        spread(m_ref)

    def phase(g, parity, s_new, m_new, s_old, m_old):
        w, u = g // UNITS, lax.rem(g, UNITS)
        w_old, u_old = (g - 1) // UNITS, lax.rem(g - 1, UNITS)
        build(w, u)
        lowest(m_new)
        keep = keepers(u_old)
        acc[...] = jnp.zeros_like(acc)

        def body(c):
            strips = []
            parts = CHUNK // PIECE
            for i in range(parts):
                score(c, i, s_new, m_new)
                strips += weigh(c, i * span // parts, (i + 1) * span // parts, s_old, m_old)
            absorb(c, strips, keep)

        chunks(body, functools.partial(run, g, parity, 1))
        finish(w_old, u_old, m_old)
        spread(m_new)

    def only_weigh(w, u, s_old, m_old):
        keep = keepers(u)
        acc[...] = jnp.zeros_like(acc)
        chunks(lambda c: absorb(c, weigh(c, 0, span, s_old, m_old), keep))
        finish(w, u, m_old)

    def relay(w, d, i):
        for side in range(2):
            h, r = i % 2, (i // 2) ^ side
            q_copy(w, side, d, h, r).wait_recv()
            if d < NEAR:
                q_copy(w, side, d + 1, h, r).start()
            if i == 0:
                t_copy(side, d).wait_recv()
                t_copy(side, d + 1).start()

    def wanted(side):
        u = slot(side, NEAR)
        step = 1 if side == 0 else ranks - 1
        return [chosen(u, lax.rem(z + i * step, ranks)) for i in range(3)]

    def narrow(w, i):
        for side in range(2):
            _, want7, want8 = wanted(side)
            r = i ^ side
            rows_of = slice(r * half * LANES, (r + 1) * half * LANES)
            first, second = (qt[w, slot(side, NEAR), h, rows_of] for h in range(2))
            if i == 0:
                sel8[w, side] = first * is_head(want8, 0).astype(BF16) + second * is_head(want8, 1).astype(BF16)
                sel8_copy(w, side).start()
            sel7[w, side, rows_of] = first * is_head(want7, 0).astype(BF16) + second * is_head(want7, 1).astype(BF16)
            sel7_copy(w, side, r).start()

    def pass_on(w):
        for side in range(2):
            sel8_copy(w, side).wait_recv()
            pass8_copy(w, side).start()
        for side in range(2):
            t_copy(side, 7).wait_recv()
        t_copy(0, 8).start()

    def arrive8(w):
        t_copy(0, 8).wait_recv()
        for side in range(2):
            pass8_copy(w, side).wait_recv()

    def arrive7(w, side):
        for r in range(2):
            sel7_copy(w, side, r).wait_recv()

    def give7(w, side):
        od7[w, side] = part[w, FAR7[side]].astype(BF16)
        for copy in far7_copies(w, side):
            copy.start()

    def give8(w):
        od8[w] = part[w, FAR8].astype(BF16)
        for side in range(2):
            for copy in far8_copies(w, side):
                copy.start()

    def pass_back(w):
        for side in range(2):
            for copy in far8_copies(w, side):
                copy.wait_recv()
            for copy in far8_passes(w, side):
                copy.start()

    def own_lse(want, h, w, u, j):
        return jnp.where(want == float(h + 1), plse[w, u, j:j + 1, :], NEG)

    def gather6(w, side):
        for copy in far7_copies(w, side) + far8_passes(w, side):
            copy.wait_recv()
        u = slot(side, NEAR)
        want6, want7, want8 = wanted(side)
        for r in range(2):
            for h in range(2):
                for k in range(half):
                    j = r * half + k
                    o, lse = mix(
                        part[w, u, j], own_lse(want6, h, w, u, j),
                        b7[w, side, j].astype(F32), jnp.where(want7 == float(h + 1), b7l[w, side, j:j + 1, :], NEG),
                    )
                    if r == side:
                        o, lse = mix(
                            o, lse, b8[w, side, k].astype(F32),
                            jnp.where(want8 == float(h + 1), b8l[w, side, j:j + 1, :], NEG),
                        )
                    chain[w, side, NEAR, h, r, k] = o.astype(BF16)
                    clse[w, side, NEAR, h, r, k:k + 1, :] = lse
                for copy in chain_copies(w, side, NEAR, h, r):
                    copy.start()

    def back(w, d, h, r):
        for side in range(2):
            for copy in chain_copies(w, side, d + 1, h, r):
                copy.wait_recv()
        for side in range(2):
            u = slot(side, d)
            want = chosen(u, z)
            for k in range(half):
                o, lse = mix(
                    chain[w, side, d, h, r, k].astype(F32), clse[w, side, d, h, r, k:k + 1, :],
                    part[w, u, r * half + k], own_lse(want, h, w, u, r * half + k),
                )
                chain[w, side, d, h, r, k] = o.astype(BF16)
                clse[w, side, d, h, r, k:k + 1, :] = lse
        for side in range(2):
            for copy in chain_copies(w, side, d, h, r):
                copy.start()

    def final(w, h, r):
        for side in range(2):
            for copy in chain_copies(w, side, 1, h, r):
                copy.wait_recv()
        for k in range(half):
            at = w * blocks + r * half + k
            o, lse = mine[h, at], mlse[h, at:at + 1, :]
            for side in range(2):
                o, lse = mix(o, lse, chain[w, side, 0, h, r, k].astype(F32), clse[w, side, 0, h, r, k:k + 1, :])
            out[columns(at), columns(h)] = jnp.transpose(o).astype(BF16)

    def causal(h):
        key_at = lax.broadcasted_iota(jnp.int32, (rows, span), 0)
        query_at = lax.broadcasted_iota(jnp.int32, (rows, span), 1)
        vt_own[h] = flipped(v_own[:, columns(h)])
        want = chosen(0, z)
        for w in range(WAVES):
            s = jnp.where(key_at <= query_at + w * span, against(k_own[:, columns(h)], qt[w, 0, h]), NEG)
            top = jnp.max(fold(s, jnp.max), axis=0, keepdims=True)
            p = jnp.exp2((s - top) * rate)
            total = jnp.sum(fold(p, jnp.sum), axis=0, keepdims=True)
            o = matmul(vt_own[h], p.astype(BF16)) * (1.0 / total)
            lse = top * rate + jnp.log2(total)
            for j in range(blocks):
                cut = slice(j * LANES, (j + 1) * LANES)
                at = w * blocks + j
                mixed, both = mix(o[:, cut], lse[:, cut], part[w, 0, j], own_lse(want, h, w, 0, j))
                mine[h, at] = mixed
                mlse[h, at:at + 1, :] = both

    steps = {}

    def place(g, step, *args):
        steps.setdefault(g, []).append(functools.partial(step, *args))

    for d in range(2, NEAR + 1):
        for i in range(4):
            place(2 * (2 * d - 3) + i, relay, 0, d, i)
    place(2 * (2 * NEAR - 3) + 1, narrow, 0, 0)
    place(2 * (2 * NEAR - 3) + 3, narrow, 0, 1)
    place(2 * 11 + 1, pass_on, 0)
    place(2 * FAR8, arrive8, 0)
    place(2 * FAR7[0], arrive7, 0, 0)
    place(2 * FAR7[1], arrive7, 0, 1)
    place(2 * FAR7[1], give8, 0)

    def run(g, parity, middle):
        for k in sorted(steps):
            if k % 2 == middle and (k // 2) % 2 == parity:

                @pl.when(g == k // 2)
                def _(k=k):
                    for step in steps[k]:
                        step()

    for c in range(n_chunks):
        vw[c, :, LANES:2 * LANES] = jnp.ones((CHUNK, LANES), BF16)
    loads[1].wait()
    for c in range(n_chunks):
        kt[c] = flipped(keys[c * CHUNK:(c + 1) * CHUNK, :])
    only_score(0, 0, s_a, m_a)
    loads[2].wait()
    for i in range(4):
        relay(0, 1, i)

    def pair(i, _):
        run(2 * i - 1, 1, 0)
        phase(2 * i - 1, 1, s_b, m_b, s_a, m_a)
        run(2 * i, 0, 0)
        phase(2 * i, 0, s_a, m_a, s_b, m_b)
        return 0

    lax.fori_loop(1, UNITS // 2, pair, 0)
    for step in steps[2 * (UNITS - 1)]:
        step()
    phase(UNITS - 1, 1, s_b, m_b, s_a, m_a)
    give7(0, 0)
    pass_back(0)
    only_weigh(0, UNITS - 1, s_b, m_b)
    give7(0, 1)
    for load in loads[3:]:
        load.wait()
    for side in range(2):
        gather6(0, side)
    for h in range(2):
        causal(h)
    order = [(h, r) for r in range(2) for h in range(2)]
    for d in range(NEAR - 1, 0, -1):
        for h, r in order:
            back(0, d, h, r)
    for h, r in order:
        final(0, h, r)

    for side in range(2):
        for d in range(1, NEAR + 2):
            t_copy(side, d).wait_send()
    t_copy(0, 8).wait_send()
    for w in range(WAVES):
        for side in range(2):
            for h in range(2):
                for r in range(2):
                    for d in range(1, NEAR + 1):
                        q_copy(w, side, d, h, r).wait_send()
                        for copy in chain_copies(w, side, d, h, r):
                            copy.wait_send()
            for copy in [sel7_copy(w, side, r) for r in range(2)] + [sel8_copy(w, side), pass8_copy(w, side)]:
                copy.wait_send()
            for copy in far8_copies(w, side) + far8_passes(w, side) + far7_copies(w, side):
                copy.wait_send()


def shards(queries, keys_own, values_own, keys_cache, values_cache, picks):
    ranks = lax.axis_size("ctx")
    rows, width = queries.shape
    depth = keys_cache.shape[0]
    span = rows // WAVES
    blocks = span // LANES
    half = blocks // 2
    rate = (width // 2) ** (-0.5) * math.log2(math.e)
    return pl.pallas_call(
        functools.partial(kernel, ranks, rate),
        out_shape=jax.ShapeDtypeStruct((rows, width), BF16),
        in_specs=[pl.BlockSpec(memory_space=pltpu.SMEM)] + [pl.BlockSpec(memory_space=pl.ANY)] * 5,
        out_specs=pl.BlockSpec(memory_space=pltpu.VMEM),
        scratch_shapes=[
            pltpu.VMEM((rows, width), BF16),
            pltpu.VMEM((rows, width), BF16),
            pltpu.VMEM((rows, width), BF16),
            pltpu.VMEM((2, LANES, rows), BF16),
            pltpu.VMEM((depth, width), BF16),
            pltpu.VMEM((depth, width), BF16),
            pltpu.VMEM((depth // CHUNK, width, CHUNK), BF16),
            pltpu.VMEM((depth // CHUNK, CHUNK, width), BF16),
            pltpu.VMEM((WAVES, UNITS, 2, span, LANES), BF16),
            pltpu.VMEM((UNITS, 8, LANES), F32),
            pltpu.VMEM((span, width), BF16),
            pltpu.VMEM((depth // CHUNK, span, CHUNK), F32),
            pltpu.VMEM((depth // CHUNK, span, CHUNK), F32),
            pltpu.VMEM((span, LANES), F32),
            pltpu.VMEM((span, LANES), F32),
            pltpu.VMEM((span, width), F32),
            pltpu.VMEM((WAVES, UNITS, blocks, LANES, LANES), F32),
            pltpu.VMEM((WAVES, UNITS, blocks, LANES), F32),
            pltpu.VMEM((2, WAVES * blocks, LANES, LANES), F32),
            pltpu.VMEM((2, WAVES * blocks, LANES), F32),
            pltpu.VMEM((WAVES, 2, span, LANES), BF16),
            pltpu.VMEM((WAVES, 2, span // 2, LANES), BF16),
            pltpu.VMEM((WAVES, 2, span // 2, LANES), BF16),
            pltpu.VMEM((WAVES, blocks, LANES, LANES), BF16),
            pltpu.VMEM((WAVES, 2, blocks, LANES, LANES), BF16),
            pltpu.VMEM((WAVES, 2, half, LANES, LANES), BF16),
            pltpu.VMEM((WAVES, 2, blocks, LANES), F32),
            pltpu.VMEM((WAVES, 2, half, LANES, LANES), BF16),
            pltpu.VMEM((WAVES, 2, blocks, LANES), F32),
            pltpu.VMEM((WAVES, 2, blocks, LANES, LANES), BF16),
            pltpu.VMEM((WAVES, 2, blocks, LANES), F32),
            pltpu.VMEM((WAVES, 2, NEAR + 1, 2, 2, half, LANES, LANES), BF16),
            pltpu.VMEM((WAVES, 2, NEAR + 1, 2, 2, half, LANES), F32),
            pltpu.SemaphoreType.DMA((5,)),
            pltpu.SemaphoreType.DMA((WAVES, 2, 8, 2, 2)),
            pltpu.SemaphoreType.DMA((WAVES, 2, 8, 2, 2)),
            pltpu.SemaphoreType.DMA((2, 8)),
            pltpu.SemaphoreType.DMA((2, 8)),
            pltpu.SemaphoreType.DMA((WAVES, 2, 6)),
            pltpu.SemaphoreType.DMA((WAVES, 2, 6)),
            pltpu.SemaphoreType.DMA((WAVES, 2, NEAR, 2, 2, 2)),
            pltpu.SemaphoreType.DMA((WAVES, 2, NEAR, 2, 2, 2)),
        ],
        compiler_params=pltpu.CompilerParams(
            collective_id=0, has_side_effects=True, vmem_limit_bytes=56 * 1024 * 1024
        ),
        cost_estimate=pl.CostEstimate(
            flops=4 * 16 * depth * rows * width, bytes_accessed=2 * (2 * depth + 4 * rows) * width,
            transcendentals=16 * depth * rows,
        ),
    )(picks, queries, keys_own, values_own, keys_cache, values_cache)


def solution(mesh):
    placed = P(("req", "ctx"), "head")
    return jax.shard_map(
        shards,
        mesh=mesh,
        in_specs=(placed,) * 5 + (P(("req", "ctx"), "head", None),),
        out_specs=placed,
        check_vma=False,
    )
```
